32 devices in a mesh: ctx: 4 (over y, core), tp: 8 (over z, x).
Axes of the slice: x: 2, y: 2, z: 4, core: 2. Of those that a mesh axis runs over, the one named last changes fastest.
Arguments:
- queries: bfloat16 [4096, 8192], P(('ctx', 'tp')), may hold values from -16 to 16
- key_tensor: bfloat16 [4096, 1024], P(('ctx', 'tp')), may hold values from -6 to 6
- value_tensor: bfloat16 [4096, 1024], P(('ctx', 'tp')), may hold values from -6 to 6
- output_gradient: bfloat16 [4096, 8192], P(('ctx', 'tp')), may hold values from -6 to 6
- key_blocks: int32 [32, 8], replicated, may hold values from 0 to 31, as said below
- slot_valid: int32 [32, 8], replicated, may hold values from 0 to 1, as said below
Outputs:
- d_q: bfloat16 [4096, 8192], P(('ctx', 'tp'))
- key_gradient: bfloat16 [4096, 1024], P(('ctx', 'tp'))
- value_gradient: bfloat16 [4096, 1024], P(('ctx', 'tp'))
The draws below stay inside these ranges and needn't reach their ends.
Inputs may be any that keep to these rules, and one draw needn't show every extreme that they name: `key_blocks`: row b names blocks b - 1, b, b + 1 (clamped to the sequence), block 0, then 8 - 4 blocks that differ from one another and from b - 1, b and b + 1. Row 0 is not read. `slot_valid`: the slot of block b itself is 1 in every row; a window slot naming a block below 1 or above 31 is 0, the block 0 slot is 1, and among the random slots a ragged leading part is 1 except where it names block 0.
All inputs are finite; a program needn't handle non-finite values.
Results may differ from the reference program's by a relative error of at most 0.006.
Values may be sent and summed in bfloat16 or wider, within the bound.
A program may use at most 256 MiB of HBM per device.

```python
import math
import jax
import jax.numpy as jnp
from jax import lax

QUERY_HEADS = 64
KEY_HEADS = 8
HEAD_SIZE = 128
BLOCK_TOKENS = 128
NB = 8
GROUP_SIZE = 8
SEQUENCE_LENGTH = 4096
BLOCK_COUNT = 32


def pair_draw(key):
    group_index = QUERY_HEADS // KEY_HEADS
    random_seed_keys = jax.random.fold_in(key, 101)
    random_seed_query = jax.random.fold_in(key, 102)
    key_row_block = jnp.clip(jax.random.normal(random_seed_keys, (SEQUENCE_LENGTH, KEY_HEADS, HEAD_SIZE), jnp.float32), -5.0, 5.0)
    query_row_block = jnp.clip(jax.random.normal(random_seed_query, (SEQUENCE_LENGTH, KEY_HEADS, group_index, HEAD_SIZE), jnp.float32), -5.0, 5.0)
    return (query_row_block.reshape(SEQUENCE_LENGTH, QUERY_HEADS * HEAD_SIZE), key_row_block.reshape(SEQUENCE_LENGTH, KEY_HEADS * HEAD_SIZE))


def one_offsets(seed_row):
    return jax.random.permutation(seed_row, BLOCK_COUNT - 3)[:NB - 4]


def list_draw(key):
    extra = NB - 4
    blocks_seq = jnp.arange(BLOCK_COUNT, dtype=jnp.int32)
    seeds_rows = jax.random.split(jax.random.fold_in(key, 201), BLOCK_COUNT)
    offsets = jax.vmap(one_offsets)(seeds_rows) + 2
    random_ids = (blocks_seq[:, None] + offsets) % BLOCK_COUNT
    counts_rows = jax.random.randint(jax.random.fold_in(key, 202), (BLOCK_COUNT, 1), 1, extra + 1)
    random_live = (jnp.arange(extra)[None, :] < counts_rows) & (random_ids != 0)
    window_ids = jnp.stack([blocks_seq - 1, blocks_seq, blocks_seq + 1], axis=1)
    window_live = jnp.stack([blocks_seq - 1 >= 1, blocks_seq >= 0, blocks_seq + 1 <= BLOCK_COUNT - 1], axis=1)
    listed = jnp.concatenate([jnp.clip(window_ids, 0, BLOCK_COUNT - 1), jnp.zeros((BLOCK_COUNT, 1), jnp.int32), random_ids.astype(jnp.int32)], axis=1)
    live_all = jnp.concatenate([window_live, (blocks_seq >= 0)[:, None], random_live], axis=1)
    return (listed.astype(jnp.int32), live_all.astype(jnp.int32))


def draw_queries(key, part):
    return pair_draw(key)[0].astype(jnp.bfloat16)


def draw_key_tensor(key, part):
    return pair_draw(key)[1].astype(jnp.bfloat16)


def draw_key_blocks(key, part):
    return list_draw(key)[0]


def draw_slot_valid(key, part):
    return list_draw(key)[1]


def levels(own_key, dims, shards, least, largest):
    def one(position, blocks):
        heights = jax.random.uniform(jax.random.fold_in(jax.random.fold_in(own_key, 6), position), (blocks,), jnp.float32, least / len(shards), largest / len(shards))
        return jnp.repeat(jnp.exp(heights), dims[position] // blocks).reshape((-1,) + (1,) * (len(dims) - position - 1))

    factor_of = one(*shards[0])
    for cut in shards[1:]:
        factor_of = factor_of * one(*cut)
    return factor_of


def normal_values(rng, extent, scale, reach, pieces=(), held_as=jnp.bfloat16):
    result = jax.random.normal(rng, extent, jnp.float32) * scale
    if len(pieces) > 0:
        result = levels(rng, extent, pieces, -0.22, 0.18) * result
    return jnp.clip(result, min=-reach, max=reach).astype(held_as)


def setup_inputs(seed: int = 0) -> dict:
    key_list = jax.random.split(jax.random.key(seed), 7)
    queries = draw_queries(jax.random.fold_in(key_list[6], 71), 0)
    key_tensor = draw_key_tensor(jax.random.fold_in(key_list[6], 71), 0)
    value_tensor = normal_values(key_list[2], (SEQUENCE_LENGTH, KEY_HEADS * HEAD_SIZE), 1.0, 6.0, ((0, 32),))
    output_gradient = normal_values(key_list[3], (SEQUENCE_LENGTH, QUERY_HEADS * HEAD_SIZE), 1.0, 6.0, ((0, 32),))
    key_blocks = draw_key_blocks(jax.random.fold_in(key_list[6], 71), 0)
    slot_valid = draw_slot_valid(jax.random.fold_in(key_list[6], 71), 0)
    return {"queries": queries, "key_tensor": key_tensor, "value_tensor": value_tensor, "output_gradient": output_gradient, "key_blocks": key_blocks, "slot_valid": slot_valid}


def block_grads(q_block, o_block, key_row_block, value_rows, live_mask):
    scaling = 1.0 / math.sqrt(HEAD_SIZE)
    scores = jnp.einsum('qgd,kd->gqk', q_block, key_row_block) * scaling
    scores = jnp.where(live_mask[None, None, :], scores, -jnp.inf)
    row_max = lax.optimization_barrier(jnp.max(scores, axis=-1, keepdims=True))
    raised = jnp.exp(scores - row_max)
    weights = raised / lax.optimization_barrier(jnp.sum(raised, axis=-1, keepdims=True))
    prob_grad = jnp.einsum('qgd,kd->gqk', o_block, value_rows)
    row_dot = lax.optimization_barrier(jnp.sum(weights * prob_grad, axis=-1, keepdims=True))
    score_grad = lax.optimization_barrier((weights * (prob_grad - row_dot)).astype(jnp.bfloat16)).astype(jnp.float32)
    rounded_weights = lax.optimization_barrier(weights.astype(jnp.bfloat16)).astype(jnp.float32)
    value_grad = jnp.einsum('gqk,qgd->kd', rounded_weights, o_block)
    key_grad = jnp.einsum('gqk,qgd->kd', score_grad, q_block) * scaling
    query_grad = jnp.einsum('gqk,kd->qgd', score_grad, key_row_block) * scaling
    return (query_grad, key_grad, value_grad)

def reference(queries, key_tensor, value_tensor, output_gradient, key_blocks, slot_valid):
    query_everything = queries.astype(jnp.float32).reshape(BLOCK_COUNT, BLOCK_TOKENS, KEY_HEADS, GROUP_SIZE, HEAD_SIZE)
    output_gradients = output_gradient.astype(jnp.float32).reshape(BLOCK_COUNT, BLOCK_TOKENS, KEY_HEADS, GROUP_SIZE, HEAD_SIZE)
    keep_rows = (jnp.arange(BLOCK_COUNT) != 0).astype(jnp.float32)
    masked_grads = output_gradients * keep_rows[:, None, None, None, None]
    key_everything = key_tensor.astype(jnp.float32).reshape(BLOCK_COUNT, BLOCK_TOKENS, KEY_HEADS, HEAD_SIZE)
    value_everything = value_tensor.astype(jnp.float32).reshape(BLOCK_COUNT, BLOCK_TOKENS, KEY_HEADS, HEAD_SIZE)
    live_rows = jnp.broadcast_to((slot_valid > 0)[:, :, None], (BLOCK_COUNT, NB, BLOCK_TOKENS)).reshape(BLOCK_COUNT, NB * BLOCK_TOKENS)
    every_key = jnp.ones((SEQUENCE_LENGTH,), jnp.int32) > 0
    query_list = []
    key_sequence = []
    value_sequence = []
    for head_index in range(KEY_HEADS):
        key_head = key_everything[:, :, head_index]
        value_head = value_everything[:, :, head_index]

        def sparse_row(packed):
            q_block, o_block, blocks, live_mask = packed
            key_row_block = key_head[blocks].reshape(NB * BLOCK_TOKENS, HEAD_SIZE)
            value_rows = value_head[blocks].reshape(NB * BLOCK_TOKENS, HEAD_SIZE)
            return block_grads(q_block, o_block, key_row_block, value_rows, live_mask)
        dq_sparse, dk_slots, dv_slots = lax.map(sparse_row, (query_everything[:, :, head_index], masked_grads[:, :, head_index], key_blocks, live_rows))
        dk_head = jnp.zeros((BLOCK_COUNT, BLOCK_TOKENS, HEAD_SIZE), jnp.float32).at[key_blocks].add(dk_slots.reshape(BLOCK_COUNT, NB, BLOCK_TOKENS, HEAD_SIZE))
        dv_head = jnp.zeros((BLOCK_COUNT, BLOCK_TOKENS, HEAD_SIZE), jnp.float32).at[key_blocks].add(dv_slots.reshape(BLOCK_COUNT, NB, BLOCK_TOKENS, HEAD_SIZE))
        dq_first, dk_first, dv_first = block_grads(query_everything[0, :, head_index], output_gradients[0, :, head_index], key_head.reshape(SEQUENCE_LENGTH, HEAD_SIZE), value_head.reshape(SEQUENCE_LENGTH, HEAD_SIZE), every_key)
        query_list.append(dq_sparse.at[0].add(dq_first))
        key_sequence.append(dk_head + dk_first.reshape(BLOCK_COUNT, BLOCK_TOKENS, HEAD_SIZE))
        value_sequence.append(dv_head + dv_first.reshape(BLOCK_COUNT, BLOCK_TOKENS, HEAD_SIZE))
    d_q = jnp.stack(query_list, axis=2).reshape(SEQUENCE_LENGTH, QUERY_HEADS * HEAD_SIZE).astype(jnp.bfloat16)
    key_gradient = jnp.stack(key_sequence, axis=2).reshape(SEQUENCE_LENGTH, KEY_HEADS * HEAD_SIZE).astype(jnp.bfloat16)
    value_gradient = jnp.stack(value_sequence, axis=2).reshape(SEQUENCE_LENGTH, KEY_HEADS * HEAD_SIZE).astype(jnp.bfloat16)
    return (d_q, key_gradient, value_gradient)
```

```python
import functools
import math

import jax
import jax.numpy as jnp
from jax import lax
from jax.experimental import pallas as pl
from jax.experimental.pallas import tpu as pltpu
from jax.sharding import PartitionSpec as P

KEY_HEADS = 8
HEAD_SIZE = 128
BLOCK_TOKENS = 128
NB = 8
GROUP_SIZE = 8

SCALE = 1.0 / math.sqrt(HEAD_SIZE)
LOG_SCALE = SCALE * math.log2(math.e)
T = BLOCK_TOKENS
D = HEAD_SIZE
F32 = jnp.float32
BF16 = jnp.bfloat16


def dot_nt(a, b):
    return lax.dot_general(a, b, (((1,), (1,)), ((), ())), preferred_element_type=F32)


def dot_nn(a, b):
    return jnp.dot(a, b, preferred_element_type=F32)


def grad_kernel(
    table, live, keep,
    q_ref, o_ref, k_ref, v_ref, qd_ref, od_ref,
    dq_ref, dk_ref, dv_ref, dqd_ref,
    kt, acc_k, acc_v, qs, os_, kg, vg, ktg, s_buf, g_buf, pb, ds,
):
    j = pl.program_id(1)
    length = k_ref.shape[0]
    chunk = math.gcd(length, 512)

    @pl.when(j == 0)
    def dense():
        qd = qd_ref[...]
        od = od_ref[...]
        rows = qd.shape[0]

        def stats(i, carry):
            m, l, dl = carry
            at = pl.multiple_of(i * chunk, chunk)
            k = k_ref[pl.ds(at, chunk), :]
            s = dot_nt(k, qd) * LOG_SCALE
            g = dot_nt(v_ref[pl.ds(at, chunk), :], od)
            kt[:, pl.ds(at, chunk)] = k.T
            m_new = jnp.maximum(m, jnp.max(s, axis=0, keepdims=True))
            f = jnp.exp2(m - m_new)
            p = jnp.exp2(s - m_new)
            l = l * f + jnp.sum(p, axis=0, keepdims=True)
            dl = dl * f + jnp.sum(p * g, axis=0, keepdims=True)
            return m_new, l, dl

        m, l, dl = lax.fori_loop(
            0, length // chunk, stats,
            (jnp.full((1, rows), -1e30, F32), jnp.zeros((1, rows), F32), jnp.zeros((1, rows), F32)),
        )
        rl = 1.0 / l
        delta = dl * rl

        def grads(i, dqt):
            at = pl.multiple_of(i * chunk, chunk)
            s = dot_nt(k_ref[pl.ds(at, chunk), :], qd) * LOG_SCALE
            g = dot_nt(v_ref[pl.ds(at, chunk), :], od)
            p = jnp.exp2(s - m) * rl
            d = (p * (g - delta)).astype(BF16)
            acc_v[pl.ds(at, chunk), :] = dot_nn(p.astype(BF16), od)
            acc_k[pl.ds(at, chunk), :] = dot_nn(d, qd)
            return dqt + dot_nn(kt[:, pl.ds(at, chunk)], d)

        dqt = lax.fori_loop(0, length // chunk, grads, jnp.zeros((D, rows), F32))
        dqd_ref[...] = (dqt * SCALE).T.astype(BF16)

    @pl.when(keep[j] == 0)
    def blank():
        dq_ref[...] = jnp.zeros_like(dq_ref)

    @pl.when(keep[j] != 0)
    def sparse():
        for g in range(GROUP_SIZE):
            qs[g * T:(g + 1) * T, :] = q_ref[:, g * D:(g + 1) * D]
            os_[g * T:(g + 1) * T, :] = o_ref[:, g * D:(g + 1) * D]
        bias = []
        for s in range(NB):
            at = pl.multiple_of(table[j * NB + s] * T, T)
            kg[s * T:(s + 1) * T, :] = k_ref[pl.ds(at, T), :]
            vg[s * T:(s + 1) * T, :] = v_ref[pl.ds(at, T), :]
            ktg[:, s * T:(s + 1) * T] = kt[:, pl.ds(at, T)]
            bias.append(jnp.where(live[j * NB + s] > 0, 0.0, -1e30).astype(F32))
        R = 2 * T
        for pair in range(GROUP_SIZE // 2):
            q2 = qs[pair * R:(pair + 1) * R, :]
            o2 = os_[pair * R:(pair + 1) * R, :]
            m = None
            for s in range(NB):
                sc = dot_nt(kg[s * T:(s + 1) * T, :], q2)
                s_buf[s * T:(s + 1) * T, :] = sc
                top = jnp.max(sc, axis=0, keepdims=True) * LOG_SCALE + bias[s]
                m = top if m is None else jnp.maximum(m, top)
            l = jnp.zeros((1, R), F32)
            dl = jnp.zeros((1, R), F32)
            for s in range(NB):
                rows = slice(s * T, (s + 1) * T)
                p = jnp.exp2(s_buf[rows, :] * LOG_SCALE - (m - bias[s]))
                g = dot_nt(vg[rows, :], o2)
                l = l + jnp.sum(p, axis=0, keepdims=True)
                dl = dl + jnp.sum(p * g, axis=0, keepdims=True)
                s_buf[rows, :] = p
                g_buf[rows, :] = g
            rl = 1.0 / l
            delta = dl * rl
            cols = slice(pair * R, (pair + 1) * R)
            for s in range(NB):
                rows = slice(s * T, (s + 1) * T)
                p = s_buf[rows, :] * rl
                pb[rows, cols] = p.astype(BF16)
                ds[rows, cols] = (p * (g_buf[rows, :] - delta)).astype(BF16)
            dqt = dot_nn(ktg[...], ds[:, cols]) * SCALE
            dq_ref[:, 2 * pair * D:(2 * pair + 1) * D] = dqt[:, :T].T.astype(BF16)
            dq_ref[:, (2 * pair + 1) * D:(2 * pair + 2) * D] = dqt[:, T:].T.astype(BF16)
        for s in range(NB):
            rows = slice(s * T, (s + 1) * T)
            at = pl.multiple_of(table[j * NB + s] * T, T)
            acc_v[pl.ds(at, T), :] += dot_nn(pb[rows, :], os_[...])
            acc_k[pl.ds(at, T), :] += dot_nn(ds[rows, :], qs[...])

    @pl.when(j == pl.num_programs(1) - 1)
    def finish():
        dk_ref[...] = (acc_k[...] * SCALE).astype(BF16)
        dv_ref[...] = acc_v[...].astype(BF16)


def gradients(table, live, keep, q, o, kv, qd, od):
    blocks = table.shape[0]
    length = kv.shape[0]
    heads = kv.shape[1] // (2 * D)
    rows = qd.shape[0]
    wide = GROUP_SIZE * D
    spec = lambda shape, index: pl.BlockSpec(shape, index)
    row_block = spec((T, wide), lambda h, j, *_: (j, h))
    once = pl.Buffered(1) if heads == 1 else None
    fixed = lambda index: pl.BlockSpec((length, D), index, pipeline_mode=once)
    dense = spec((rows, D), lambda h, j, *_: (0, h))
    return pl.pallas_call(
        grad_kernel,
        grid_spec=pltpu.PrefetchScalarGridSpec(
            num_scalar_prefetch=3,
            grid=(heads, blocks),
            in_specs=[
                row_block, row_block,
                fixed(lambda h, j, *_: (0, h)),
                fixed(lambda h, j, *_: (0, heads + h)),
                dense, dense,
            ],
            out_specs=[
                row_block,
                spec((length, D), lambda h, j, *_: (0, h)),
                spec((length, D), lambda h, j, *_: (0, h)),
                dense,
            ],
            scratch_shapes=[
                pltpu.VMEM((D, length), BF16),
                pltpu.VMEM((length, D), F32),
                pltpu.VMEM((length, D), F32),
                pltpu.VMEM((wide, D), BF16),
                pltpu.VMEM((wide, D), BF16),
                pltpu.VMEM((NB * T, D), BF16),
                pltpu.VMEM((NB * T, D), BF16),
                pltpu.VMEM((D, NB * T), BF16),
                pltpu.VMEM((NB * T, 2 * T), F32),
                pltpu.VMEM((NB * T, 2 * T), F32),
                pltpu.VMEM((NB * T, wide), BF16),
                pltpu.VMEM((NB * T, wide), BF16),
            ],
        ),
        out_shape=[
            jax.ShapeDtypeStruct(q.shape, BF16),
            jax.ShapeDtypeStruct((length, heads * D), BF16),
            jax.ShapeDtypeStruct((length, heads * D), BF16),
            jax.ShapeDtypeStruct(qd.shape, BF16),
        ],
        compiler_params=pltpu.CompilerParams(
            dimension_semantics=("arbitrary", "arbitrary"),
            vmem_limit_bytes=60 * 1024 * 1024,
        ),
        cost_estimate=pl.CostEstimate(
            flops=10 * heads * (blocks + 1) * (wide * NB * T * D),
            bytes_accessed=4 * q.size * 2 + 4 * kv.size * 2,
            transcendentals=heads * (blocks + 1) * wide * NB * T,
        ),
    )(table.reshape(-1), live.reshape(-1), keep, q, o, kv, kv, qd, od)


def tables(key_blocks, slot_valid, ctx, tp, pieces):
    t = lax.axis_index("tp")
    pick = lambda a: lax.dynamic_slice_in_dim(
        a.reshape(ctx, tp * pieces, NB), t * pieces, pieces, 1
    ).reshape(ctx * pieces, NB)
    blocks = pick(key_blocks)
    owner = blocks // pieces
    place = ((owner % tp) * ctx + owner // tp) * pieces + blocks % pieces
    number = jnp.arange(ctx * pieces)
    own = ((number // pieces) * tp + t) * pieces + number % pieces
    return place.astype(jnp.int32), pick(slot_valid), (own != 0).astype(jnp.int32)


def per_device(queries, key_tensor, value_tensor, output_gradient, key_blocks, slot_valid):
    ctx = lax.axis_size("ctx")
    tp = lax.axis_size("tp")
    tokens = queries.shape[0]
    pieces = tokens // T
    heads = KEY_HEADS // ctx
    rows = GROUP_SIZE * T // tp
    wide = GROUP_SIZE * D
    tp_index = lax.axis_index("tp")
    swap = functools.partial(lax.all_to_all, axis_name="ctx", tiled=True)
    kv = jnp.concatenate(
        [key_tensor.reshape(tokens, ctx, heads * D), value_tensor.reshape(tokens, ctx, heads * D)], axis=2
    ).reshape(tokens, ctx * 2 * heads * D)
    kv = swap(kv, split_axis=1, concat_axis=0)
    kv = lax.all_gather(kv, "tp", axis=0, tiled=True)
    q = swap(queries, split_axis=1, concat_axis=0)
    o = swap(output_gradient, split_axis=1, concat_axis=0)

    def spread(a):
        a = a[:T].reshape(T, heads, GROUP_SIZE, D).transpose(2, 0, 1, 3).reshape(GROUP_SIZE * T, heads * D)
        return lax.all_to_all(a, "tp", split_axis=0, concat_axis=0, tiled=True)[:rows]

    table, live, keep = tables(key_blocks, slot_valid, ctx, tp, pieces)
    dq, dk, dv, dqd = gradients(table, live, keep, q, o, kv, spread(q), spread(o))
    first = lax.all_gather(dqd, "tp", axis=0, tiled=True)
    first = first.reshape(GROUP_SIZE, T, heads, D).transpose(1, 2, 0, 3).reshape(T, heads * wide)
    dq = lax.dynamic_update_slice(dq, jnp.where(tp_index == 0, first, dq[:T]), (0, 0))
    back = lambda a: swap(a, split_axis=0, concat_axis=1)

    def collect(a):
        a = lax.all_to_all(a, "tp", split_axis=0, concat_axis=0, tiled=True)
        return jnp.sum(a.reshape(tp, ctx * tokens, heads * D).astype(F32), axis=0).astype(BF16)

    return back(dq), back(collect(dk)), back(collect(dv))


def solution(mesh):
    rows = P(("ctx", "tp"), None)
    return jax.shard_map(
        per_device,
        mesh=mesh,
        in_specs=(rows, rows, rows, rows, P(), P()),
        out_specs=(rows, rows, rows),
        check_vma=False,
    )
```

```python
import functools
import math

import jax
import jax.numpy as jnp
from jax import lax
from jax.experimental import pallas as pl
from jax.experimental.pallas import tpu as pltpu
from jax.sharding import PartitionSpec as P

KEY_HEADS = 8
HEAD_SIZE = 128
BLOCK_TOKENS = 128
NB = 8
GROUP_SIZE = 8
SUB = 2

SCALE = 1.0 / math.sqrt(HEAD_SIZE)
LOG_SCALE = SCALE * math.log2(math.e)
T = BLOCK_TOKENS
D = HEAD_SIZE
F32 = jnp.float32
BF16 = jnp.bfloat16


def dot_nt(a, b):
    return lax.dot_general(a, b, (((1,), (1,)), ((), ())), preferred_element_type=F32)


def dot_nn(a, b):
    return jnp.dot(a, b, preferred_element_type=F32)


def grad_kernel(
    table, live, keep,
    q_ref, o_ref, k_ref, v_ref, qd_ref, od_ref,
    dq_ref, dk_ref, dv_ref, dqd_ref,
    kt, acc_k, acc_v, qs, os_, kg, vg, ktg, s_buf, g_buf, pb, ds,
):
    j = pl.program_id(1)
    length = k_ref.shape[0]
    chunk = math.gcd(length, 512)

    @pl.when(j == 0)
    def dense():
        qd = qd_ref[...]
        od = od_ref[...]
        rows = qd.shape[0]

        def stats(i, carry):
            m, l, dl = carry
            at = pl.multiple_of(i * chunk, chunk)
            k = k_ref[pl.ds(at, chunk), :]
            s = dot_nt(k, qd) * LOG_SCALE
            g = dot_nt(v_ref[pl.ds(at, chunk), :], od)
            kt[:, pl.ds(at, chunk)] = k.T
            m_new = jnp.maximum(m, jnp.max(s, axis=0, keepdims=True))
            f = jnp.exp2(m - m_new)
            p = jnp.exp2(s - m_new)
            l = l * f + jnp.sum(p, axis=0, keepdims=True)
            dl = dl * f + jnp.sum(p * g, axis=0, keepdims=True)
            return m_new, l, dl

        m, l, dl = lax.fori_loop(
            0, length // chunk, stats,
            (jnp.full((1, rows), -1e30, F32), jnp.zeros((1, rows), F32), jnp.zeros((1, rows), F32)),
        )
        rl = 1.0 / l
        delta = dl * rl

        def grads(i, dqt):
            at = pl.multiple_of(i * chunk, chunk)
            s = dot_nt(k_ref[pl.ds(at, chunk), :], qd) * LOG_SCALE
            g = dot_nt(v_ref[pl.ds(at, chunk), :], od)
            p = jnp.exp2(s - m) * rl
            d = (p * (g - delta)).astype(BF16)
            acc_v[pl.ds(at, chunk), :] = dot_nn(p.astype(BF16), od)
            acc_k[pl.ds(at, chunk), :] = dot_nn(d, qd)
            return dqt + dot_nn(kt[:, pl.ds(at, chunk)], d)

        dqt = lax.fori_loop(0, length // chunk, grads, jnp.zeros((D, rows), F32))
        dqd_ref[...] = (dqt * SCALE).T.astype(BF16)

    @pl.when(keep[j] == 0)
    def blank():
        dq_ref[...] = jnp.zeros_like(dq_ref)

    @pl.when(keep[j] != 0)
    def sparse():
        for g in range(GROUP_SIZE):
            qs[g * T:(g + 1) * T, :] = q_ref[:, g * D:(g + 1) * D]
            os_[g * T:(g + 1) * T, :] = o_ref[:, g * D:(g + 1) * D]
        bias = []
        for s in range(NB):
            at = pl.multiple_of(table[j * NB + s] * T, T)
            kg[s * T:(s + 1) * T, :] = k_ref[pl.ds(at, T), :]
            vg[s * T:(s + 1) * T, :] = v_ref[pl.ds(at, T), :]
            ktg[:, s * T:(s + 1) * T] = kt[:, pl.ds(at, T)]
            bias.append(jnp.where(live[j * NB + s] > 0, 0.0, -1e30).astype(F32))
        R = 2 * T
        for pair in range(GROUP_SIZE // 2):
            q2 = qs[pair * R:(pair + 1) * R, :]
            o2 = os_[pair * R:(pair + 1) * R, :]
            m = None
            for s in range(NB):
                sc = dot_nt(kg[s * T:(s + 1) * T, :], q2)
                s_buf[s * T:(s + 1) * T, :] = sc
                top = jnp.max(sc, axis=0, keepdims=True) * LOG_SCALE + bias[s]
                m = top if m is None else jnp.maximum(m, top)
            l = jnp.zeros((1, R), F32)
            dl = jnp.zeros((1, R), F32)
            for s in range(NB):
                rows = slice(s * T, (s + 1) * T)
                p = jnp.exp2(s_buf[rows, :] * LOG_SCALE - (m - bias[s]))
                g = dot_nt(vg[rows, :], o2)
                l = l + jnp.sum(p, axis=0, keepdims=True)
                dl = dl + jnp.sum(p * g, axis=0, keepdims=True)
                s_buf[rows, :] = p
                g_buf[rows, :] = g
            rl = 1.0 / l
            delta = dl * rl
            cols = slice(pair * R, (pair + 1) * R)
            for s in range(NB):
                rows = slice(s * T, (s + 1) * T)
                p = s_buf[rows, :] * rl
                pb[rows, cols] = p.astype(BF16)
                ds[rows, cols] = (p * (g_buf[rows, :] - delta)).astype(BF16)
            dqt = dot_nn(ktg[...], ds[:, cols]) * SCALE
            dq_ref[:, 2 * pair * D:(2 * pair + 1) * D] = dqt[:, :T].T.astype(BF16)
            dq_ref[:, (2 * pair + 1) * D:(2 * pair + 2) * D] = dqt[:, T:].T.astype(BF16)
        for s in range(NB):
            rows = slice(s * T, (s + 1) * T)
            at = pl.multiple_of(table[j * NB + s] * T, T)
            acc_v[pl.ds(at, T), :] += dot_nn(pb[rows, :], os_[...])
            acc_k[pl.ds(at, T), :] += dot_nn(ds[rows, :], qs[...])

    @pl.when(j == pl.num_programs(1) - 1)
    def finish():
        dk_ref[...] = (acc_k[...] * SCALE).astype(BF16)
        dv_ref[...] = acc_v[...].astype(BF16)


def gradients(table, live, keep, q, o, kv, qd, od):
    blocks = table.shape[0]
    length = kv.shape[0]
    heads = kv.shape[1] // (2 * D)
    rows = qd.shape[0]
    wide = GROUP_SIZE * D
    spec = lambda shape, index: pl.BlockSpec(shape, index)
    row_block = spec((T, wide), lambda h, j, *_: (j, h))
    once = pl.Buffered(1) if heads == 1 else None
    fixed = lambda index: pl.BlockSpec((length, D), index, pipeline_mode=once)
    dense = spec((rows, D), lambda h, j, *_: (0, h))
    return pl.pallas_call(
        grad_kernel,
        grid_spec=pltpu.PrefetchScalarGridSpec(
            num_scalar_prefetch=3,
            grid=(heads, blocks),
            in_specs=[
                row_block, row_block,
                fixed(lambda h, j, *_: (0, h)),
                fixed(lambda h, j, *_: (0, heads + h)),
                dense, dense,
            ],
            out_specs=[
                row_block,
                spec((length, D), lambda h, j, *_: (0, h)),
                spec((length, D), lambda h, j, *_: (0, h)),
                dense,
            ],
            scratch_shapes=[
                pltpu.VMEM((D, length), BF16),
                pltpu.VMEM((length, D), F32),
                pltpu.VMEM((length, D), F32),
                pltpu.VMEM((wide, D), BF16),
                pltpu.VMEM((wide, D), BF16),
                pltpu.VMEM((NB * T, D), BF16),
                pltpu.VMEM((NB * T, D), BF16),
                pltpu.VMEM((D, NB * T), BF16),
                pltpu.VMEM((NB * T, 2 * T), F32),
                pltpu.VMEM((NB * T, 2 * T), F32),
                pltpu.VMEM((NB * T, wide), BF16),
                pltpu.VMEM((NB * T, wide), BF16),
            ],
        ),
        out_shape=[
            jax.ShapeDtypeStruct(q.shape, BF16),
            jax.ShapeDtypeStruct((length, heads * D), BF16),
            jax.ShapeDtypeStruct((length, heads * D), BF16),
            jax.ShapeDtypeStruct(qd.shape, BF16),
        ],
        compiler_params=pltpu.CompilerParams(
            dimension_semantics=("arbitrary", "arbitrary"),
            vmem_limit_bytes=60 * 1024 * 1024,
        ),
        cost_estimate=pl.CostEstimate(
            flops=10 * heads * (blocks + 1) * (wide * NB * T * D),
            bytes_accessed=4 * q.size * 2 + 4 * kv.size * 2,
            transcendentals=heads * (blocks + 1) * wide * NB * T,
        ),
    )(table.reshape(-1), live.reshape(-1), keep, q, o, kv, kv, qd, od)


def tables(key_blocks, slot_valid, ctx, tp, pieces):
    t = lax.axis_index("tp")
    pick = lambda a: lax.dynamic_slice_in_dim(
        a.reshape(ctx, tp * pieces, NB), t * pieces, pieces, 1
    ).reshape(ctx * pieces, NB)
    blocks = pick(key_blocks)
    owner = blocks // pieces
    place = ((owner % tp) * ctx + owner // tp) * pieces + blocks % pieces
    number = jnp.arange(ctx * pieces)
    own = ((number // pieces) * tp + t) * pieces + number % pieces
    return place.astype(jnp.int32), pick(slot_valid), (own != 0).astype(jnp.int32)


def ring_place(t, n):
    odd = t % 2
    return (1 - odd) * (t // 2) + odd * (n - 1 - t // 2)


def ring_owner(p, n):
    p = (p + 2 * n) % n
    far = p // (n // 2)
    return (1 - far) * 2 * p + far * (2 * (n - 1 - p) + 1)


def signal(sem, c, t):
    pl.semaphore_signal(sem, inc=1, device_id=(c, t), device_id_type=pl.DeviceIdType.MESH)


def meet(c, t, ctx, tp, before, after):
    barrier = pltpu.get_barrier_semaphore()
    for k in range(1, ctx):
        signal(barrier, (c + k) % ctx, t)
    signal(barrier, c, before)
    signal(barrier, c, after)
    origin = c * tp + t == 0

    @pl.when(origin)
    def greet():
        def one(i, none):
            signal(barrier, i // tp, i % tp)
            return none

        lax.fori_loop(1, ctx * tp, one, 0)
        pl.semaphore_wait(barrier, ctx + 1 + ctx * tp - 1)

    @pl.when(jnp.logical_not(origin))
    def answer():
        signal(barrier, 0, 0)
        pl.semaphore_wait(barrier, ctx + 2)

    return origin


def remote(src, dst, send, recv, c, t):
    return pltpu.make_async_remote_copy(
        src_ref=src, dst_ref=dst, send_sem=send, recv_sem=recv,
        device_id=(c, t), device_id_type=pl.DeviceIdType.MESH,
    )


def await_bytes(ref, sem):
    pltpu.make_async_copy(ref, ref, sem).wait()


def return_kernel(
    ctx, tp,
    dq_ref, dqd_ref, dk_ref, dv_ref,
    dq_out, dk_out, dv_out,
    got, done, ring_send, ring_recv, q_send, q_recv, d_send, g_send, g_recv,
):
    c = lax.axis_index("ctx")
    t = lax.axis_index("tp")
    tokens = dq_out.shape[0]
    width = dq_ref.shape[1]
    thin = dk_ref.shape[1]
    heads = thin // D
    chunk = ctx * tokens
    part = chunk // SUB
    p = ring_place(t, tp)
    after = ring_owner(p + 1, tp)
    before = ring_owner(p - 1, tp)
    origin = meet(c, t, ctx, tp, before, after)
    ways = ((dk_ref, 1, after), (dv_ref, -1, before))

    def own(way, place, sub):
        at = pl.multiple_of(ring_owner(place, tp) * chunk + sub * part, part)
        return ways[way][0].at[pl.ds(at, part), :]

    def hop(way, src, step, sub):
        return remote(
            src, got.at[way, step, sub], ring_send.at[way, step, sub],
            ring_recv.at[way, step, sub], c, ways[way][2],
        )

    for sub in range(SUB):
        for way in range(2):
            hop(way, own(way, p - ways[way][1], sub), 0, sub).start()

    def rows_of(k):
        return dq_ref.at[pl.ds(pl.multiple_of(k * tokens, tokens), tokens), :]

    columns = dq_out.at[:, pl.ds(pl.multiple_of(c * width, width), width)]
    for k in range(1, ctx):
        peer = (c + k) % ctx

        @pl.when(peer * tp + t != 0)
        def send():
            remote(rows_of(peer), columns, q_send.at[k], q_recv, peer, t).start()

    @pl.when(jnp.logical_not(origin))
    def keep_rows():
        pltpu.make_async_copy(rows_of(c), columns, q_recv).start()

    rows = dqd_ref.shape[0]
    first = t * rows
    token = pl.multiple_of(first % T, rows)

    def dense(h):
        column = c * width + h * (GROUP_SIZE * D) + (first // T) * D
        return (
            dqd_ref.at[:, h * D:(h + 1) * D],
            dq_out.at[pl.ds(token, rows), pl.ds(pl.multiple_of(column, D), D)],
        )

    for h in range(heads):
        src, dst = dense(h)

        @pl.when(origin)
        def stay():
            pltpu.make_async_copy(src, dst, q_recv).start()

        @pl.when(jnp.logical_not(origin))
        def leave():
            remote(src, dst, d_send.at[h], q_recv, 0, 0).start()

    def total(way, step, sub):
        hop(way, got.at[way, step, sub], step, sub).wait_recv()
        place = p - ways[way][1] * (step + 2)
        return got[way, step, sub].astype(F32) + own(way, place, sub)[...].astype(F32)

    def advance(step, none):
        for sub in range(SUB):
            for way in range(2):
                got[way, step - 1, sub] = total(way, step - 1, sub).astype(BF16)
                hop(way, got.at[way, step - 1, sub], step, sub).start()
        return none

    lax.fori_loop(1, tp - 1, advance, 0)
    outs = (dk_out, dv_out)

    def give(way, peer, k):
        src = done.at[way, pl.ds(pl.multiple_of(peer * tokens, tokens), tokens), :]
        dst = outs[way].at[:, pl.ds(pl.multiple_of(c * thin, thin), thin)]
        return src, dst

    for sub in range(SUB):
        for way in range(2):
            done[way, sub * part:(sub + 1) * part, :] = total(way, tp - 2, sub).astype(BF16)
    for way in range(2):
        for k in range(1, ctx):
            peer = (c + k) % ctx
            src, dst = give(way, peer, k)
            remote(src, dst, g_send.at[way, k], g_recv.at[way], peer, t).start()
        src, dst = give(way, c, 0)
        pltpu.make_async_copy(src, dst, g_recv.at[way]).start()

    await_bytes(dq_out, q_recv)
    for way in range(2):
        await_bytes(outs[way], g_recv.at[way])
    for way in range(2):
        for k in range(1, ctx):
            peer = (c + k) % ctx
            src, dst = give(way, peer, k)
            remote(src, dst, g_send.at[way, k], g_recv.at[way], peer, t).wait_send()
    for k in range(1, ctx):
        peer = (c + k) % ctx

        @pl.when(peer * tp + t != 0)
        def sent():
            remote(rows_of(peer), columns, q_send.at[k], q_recv, peer, t).wait_send()

    for h in range(heads):
        src, dst = dense(h)

        @pl.when(jnp.logical_not(origin))
        def left():
            remote(src, dst, d_send.at[h], q_recv, 0, 0).wait_send()

    def settle(step, none):
        for sub in range(SUB):
            for way in range(2):
                hop(way, got.at[way, step, sub], step, sub).wait_send()
        return none

    lax.fori_loop(0, tp - 1, settle, 0)


def send_back(dq, dqd, dk, dv, ctx, tp):
    tokens = dq.shape[0] // ctx
    thin = dk.shape[1]
    heads = thin // D
    part = ctx * tokens // SUB
    anywhere = pl.BlockSpec(memory_space=pl.ANY)
    vmem = pl.BlockSpec(memory_space=pltpu.VMEM)
    dma = pltpu.SemaphoreType.DMA
    return pl.pallas_call(
        functools.partial(return_kernel, ctx, tp),
        in_specs=[anywhere, anywhere, vmem, vmem],
        out_specs=[anywhere, anywhere, anywhere],
        out_shape=[
            jax.ShapeDtypeStruct((tokens, ctx * dq.shape[1]), BF16),
            jax.ShapeDtypeStruct((tokens, ctx * thin), BF16),
            jax.ShapeDtypeStruct((tokens, ctx * thin), BF16),
        ],
        scratch_shapes=[
            pltpu.VMEM((2, tp - 1, SUB, part, thin), BF16),
            pltpu.VMEM((2, ctx * tokens, thin), BF16),
            dma((2, tp - 1, SUB)), dma((2, tp - 1, SUB)),
            dma((ctx,)), dma, dma((heads,)), dma((2, ctx)), dma((2,)),
        ],
        compiler_params=pltpu.CompilerParams(
            collective_id=1, has_side_effects=True, vmem_limit_bytes=48 * 1024 * 1024
        ),
    )(dq, dqd, dk, dv)


def per_device(queries, key_tensor, value_tensor, output_gradient, key_blocks, slot_valid):
    ctx = lax.axis_size("ctx")
    tp = lax.axis_size("tp")
    tokens = queries.shape[0]
    pieces = tokens // T
    heads = KEY_HEADS // ctx
    rows = GROUP_SIZE * T // tp
    swap = functools.partial(lax.all_to_all, axis_name="ctx", tiled=True)
    kv = jnp.concatenate(
        [key_tensor.reshape(tokens, ctx, heads * D), value_tensor.reshape(tokens, ctx, heads * D)], axis=2
    ).reshape(tokens, ctx * 2 * heads * D)
    kv = swap(kv, split_axis=1, concat_axis=0)
    kv = lax.all_gather(kv, "tp", axis=0, tiled=True)
    q = swap(queries, split_axis=1, concat_axis=0)
    o = swap(output_gradient, split_axis=1, concat_axis=0)

    def spread(a):
        a = a[:T].reshape(T, heads, GROUP_SIZE, D).transpose(2, 0, 1, 3).reshape(GROUP_SIZE * T, heads * D)
        return lax.all_to_all(a, "tp", split_axis=0, concat_axis=0, tiled=True)[:rows]

    table, live, keep = tables(key_blocks, slot_valid, ctx, tp, pieces)
    dq, dk, dv, dqd = gradients(table, live, keep, q, o, kv, spread(q), spread(o))
    return tuple(send_back(dq, dqd, dk, dv, ctx, tp))


def solution(mesh):
    rows = P(("ctx", "tp"), None)
    return jax.shard_map(
        per_device,
        mesh=mesh,
        in_specs=(rows, rows, rows, rows, P(), P()),
        out_specs=(rows, rows, rows),
        check_vma=False,
    )
```

```python
import functools
import math

import jax
import jax.numpy as jnp
from jax import lax
from jax.experimental import pallas as pl
from jax.experimental.pallas import tpu as pltpu
from jax.sharding import PartitionSpec as P

KEY_HEADS = 8
HEAD_SIZE = 128
BLOCK_TOKENS = 128
NB = 8
GROUP_SIZE = 8
SUB = 2

SCALE = 1.0 / math.sqrt(HEAD_SIZE)
LOG_SCALE = SCALE * math.log2(math.e)
T = BLOCK_TOKENS
D = HEAD_SIZE
F32 = jnp.float32
BF16 = jnp.bfloat16


def dot_nt(a, b):
    return lax.dot_general(a, b, (((1,), (1,)), ((), ())), preferred_element_type=F32)


def dot_nn(a, b):
    return jnp.dot(a, b, preferred_element_type=F32)


def grad_kernel(
    table, live, keep,
    q_ref, o_ref, k_ref, v_ref, qd_ref, od_ref,
    dq_ref, dk_ref, dv_ref, dqd_ref,
    kt, acc_k, acc_v, qs, os_, kg, vg, ktg, s_buf, g_buf, pb, ds,
):
    j = pl.program_id(1)
    length = k_ref.shape[0]
    chunk = math.gcd(length, 512)

    @pl.when(j == 0)
    def dense():
        qd = qd_ref[...]
        od = od_ref[...]
        rows = qd.shape[0]

        def stats(i, carry):
            m, l, dl = carry
            at = pl.multiple_of(i * chunk, chunk)
            k = k_ref[pl.ds(at, chunk), :]
            s = dot_nt(k, qd) * LOG_SCALE
            g = dot_nt(v_ref[pl.ds(at, chunk), :], od)
            kt[:, pl.ds(at, chunk)] = k.T
            m_new = jnp.maximum(m, jnp.max(s, axis=0, keepdims=True))
            f = jnp.exp2(m - m_new)
            p = jnp.exp2(s - m_new)
            l = l * f + jnp.sum(p, axis=0, keepdims=True)
            dl = dl * f + jnp.sum(p * g, axis=0, keepdims=True)
            return m_new, l, dl

        m, l, dl = lax.fori_loop(
            0, length // chunk, stats,
            (jnp.full((1, rows), -1e30, F32), jnp.zeros((1, rows), F32), jnp.zeros((1, rows), F32)),
        )
        rl = 1.0 / l
        delta = dl * rl

        def grads(i, dqt):
            at = pl.multiple_of(i * chunk, chunk)
            s = dot_nt(k_ref[pl.ds(at, chunk), :], qd) * LOG_SCALE
            g = dot_nt(v_ref[pl.ds(at, chunk), :], od)
            p = jnp.exp2(s - m) * rl
            d = (p * (g - delta)).astype(BF16)
            acc_v[pl.ds(at, chunk), :] = dot_nn(p.astype(BF16), od)
            acc_k[pl.ds(at, chunk), :] = dot_nn(d, qd)
            return dqt + dot_nn(kt[:, pl.ds(at, chunk)], d)

        dqt = lax.fori_loop(0, length // chunk, grads, jnp.zeros((D, rows), F32))
        dqd_ref[...] = (dqt * SCALE).T.astype(BF16)

    @pl.when(keep[j] == 0)
    def blank():
        dq_ref[...] = jnp.zeros_like(dq_ref)

    @pl.when(keep[j] != 0)
    def sparse():
        for g in range(GROUP_SIZE):
            qs[g * T:(g + 1) * T, :] = q_ref[:, g * D:(g + 1) * D]
            os_[g * T:(g + 1) * T, :] = o_ref[:, g * D:(g + 1) * D]
        bias = []
        for s in range(NB):
            at = pl.multiple_of(table[j * NB + s] * T, T)
            kg[s * T:(s + 1) * T, :] = k_ref[pl.ds(at, T), :]
            vg[s * T:(s + 1) * T, :] = v_ref[pl.ds(at, T), :]
            ktg[:, s * T:(s + 1) * T] = kt[:, pl.ds(at, T)]
            bias.append(jnp.where(live[j * NB + s] > 0, 0.0, -1e30).astype(F32))
        R = 2 * T
        for pair in range(GROUP_SIZE // 2):
            q2 = qs[pair * R:(pair + 1) * R, :]
            o2 = os_[pair * R:(pair + 1) * R, :]
            m = None
            for s in range(NB):
                sc = dot_nt(kg[s * T:(s + 1) * T, :], q2)
                s_buf[s * T:(s + 1) * T, :] = sc
                top = jnp.max(sc, axis=0, keepdims=True) * LOG_SCALE + bias[s]
                m = top if m is None else jnp.maximum(m, top)
            l = jnp.zeros((1, R), F32)
            dl = jnp.zeros((1, R), F32)
            for s in range(NB):
                rows = slice(s * T, (s + 1) * T)
                p = jnp.exp2(s_buf[rows, :] * LOG_SCALE - (m - bias[s]))
                g = dot_nt(vg[rows, :], o2)
                l = l + jnp.sum(p, axis=0, keepdims=True)
                dl = dl + jnp.sum(p * g, axis=0, keepdims=True)
                s_buf[rows, :] = p
                g_buf[rows, :] = g
            rl = 1.0 / l
            delta = dl * rl
            cols = slice(pair * R, (pair + 1) * R)
            for s in range(NB):
                rows = slice(s * T, (s + 1) * T)
                p = s_buf[rows, :] * rl
                pb[rows, cols] = p.astype(BF16)
                ds[rows, cols] = (p * (g_buf[rows, :] - delta)).astype(BF16)
            dqt = dot_nn(ktg[...], ds[:, cols]) * SCALE
            dq_ref[:, 2 * pair * D:(2 * pair + 1) * D] = dqt[:, :T].T.astype(BF16)
            dq_ref[:, (2 * pair + 1) * D:(2 * pair + 2) * D] = dqt[:, T:].T.astype(BF16)
        for s in range(NB):
            rows = slice(s * T, (s + 1) * T)
            at = pl.multiple_of(table[j * NB + s] * T, T)
            acc_v[pl.ds(at, T), :] += dot_nn(pb[rows, :], os_[...])
            acc_k[pl.ds(at, T), :] += dot_nn(ds[rows, :], qs[...])

    @pl.when(j == pl.num_programs(1) - 1)
    def finish():
        dk_ref[...] = (acc_k[...] * SCALE).astype(BF16)
        dv_ref[...] = acc_v[...].astype(BF16)


def gradients(table, live, keep, q, o, k, v, qd, od):
    blocks = table.shape[0]
    length = k.shape[0]
    heads = k.shape[1] // D
    rows = qd.shape[0]
    wide = GROUP_SIZE * D
    spec = lambda shape, index: pl.BlockSpec(shape, index)
    row_block = spec((T, wide), lambda h, j, *_: (j, h))
    once = pl.Buffered(1) if heads == 1 else None
    fixed = lambda index: pl.BlockSpec((length, D), index, pipeline_mode=once)
    dense = spec((rows, D), lambda h, j, *_: (0, h))
    return pl.pallas_call(
        grad_kernel,
        grid_spec=pltpu.PrefetchScalarGridSpec(
            num_scalar_prefetch=3,
            grid=(heads, blocks),
            in_specs=[
                row_block, row_block,
                fixed(lambda h, j, *_: (0, h)),
                fixed(lambda h, j, *_: (0, h)),
                dense, dense,
            ],
            out_specs=[
                row_block,
                spec((length, D), lambda h, j, *_: (0, h)),
                spec((length, D), lambda h, j, *_: (0, h)),
                dense,
            ],
            scratch_shapes=[
                pltpu.VMEM((D, length), BF16),
                pltpu.VMEM((length, D), F32),
                pltpu.VMEM((length, D), F32),
                pltpu.VMEM((wide, D), BF16),
                pltpu.VMEM((wide, D), BF16),
                pltpu.VMEM((NB * T, D), BF16),
                pltpu.VMEM((NB * T, D), BF16),
                pltpu.VMEM((D, NB * T), BF16),
                pltpu.VMEM((NB * T, 2 * T), F32),
                pltpu.VMEM((NB * T, 2 * T), F32),
                pltpu.VMEM((NB * T, wide), BF16),
                pltpu.VMEM((NB * T, wide), BF16),
            ],
        ),
        out_shape=[
            jax.ShapeDtypeStruct(q.shape, BF16),
            jax.ShapeDtypeStruct((length, heads * D), BF16),
            jax.ShapeDtypeStruct((length, heads * D), BF16),
            jax.ShapeDtypeStruct(qd.shape, BF16),
        ],
        compiler_params=pltpu.CompilerParams(
            dimension_semantics=("arbitrary", "arbitrary"),
            vmem_limit_bytes=60 * 1024 * 1024,
        ),
        cost_estimate=pl.CostEstimate(
            flops=10 * heads * (blocks + 1) * (wide * NB * T * D),
            bytes_accessed=6 * q.size + 8 * k.size,
            transcendentals=heads * (blocks + 1) * wide * NB * T,
        ),
    )(table.reshape(-1), live.reshape(-1), keep, q, o, k, v, qd, od)


def tables(key_blocks, slot_valid, ctx, tp, pieces):
    t = lax.axis_index("tp")
    pick = lambda a: lax.dynamic_slice_in_dim(
        a.reshape(ctx, tp * pieces, NB), t * pieces, pieces, 1
    ).reshape(ctx * pieces, NB)
    blocks = pick(key_blocks)
    owner = blocks // pieces
    place = ((owner % tp) * ctx + owner // tp) * pieces + blocks % pieces
    number = jnp.arange(ctx * pieces)
    own = ((number // pieces) * tp + t) * pieces + number % pieces
    return place.astype(jnp.int32), pick(slot_valid), (own != 0).astype(jnp.int32)


def ring_place(t, n):
    odd = t % 2
    return (1 - odd) * (t // 2) + odd * (n - 1 - t // 2)


def ring_owner(p, n):
    p = (p + 2 * n) % n
    far = p // (n // 2)
    return (1 - far) * 2 * p + far * (2 * (n - 1 - p) + 1)


def signal(sem, c, t):
    pl.semaphore_signal(sem, inc=1, device_id=(c, t), device_id_type=pl.DeviceIdType.MESH)


def meet(c, t, ctx, tp, before, after):
    barrier = pltpu.get_barrier_semaphore()
    for k in range(1, ctx):
        signal(barrier, (c + k) % ctx, t)
    signal(barrier, c, before)
    signal(barrier, c, after)
    origin = c * tp + t == 0

    @pl.when(origin)
    def greet():
        def one(i, none):
            signal(barrier, i // tp, i % tp)
            return none

        lax.fori_loop(1, ctx * tp, one, 0)
        pl.semaphore_wait(barrier, ctx + 1 + ctx * tp - 1)

    @pl.when(jnp.logical_not(origin))
    def answer():
        signal(barrier, 0, 0)
        pl.semaphore_wait(barrier, ctx + 2)

    return origin


def remote(src, dst, send, recv, c, t):
    return pltpu.make_async_remote_copy(
        src_ref=src, dst_ref=dst, send_sem=send, recv_sem=recv,
        device_id=(c, t), device_id_type=pl.DeviceIdType.MESH,
    )


def await_bytes(ref, sem):
    pltpu.make_async_copy(ref, ref, sem).wait()


def return_kernel(
    ctx, tp,
    dq_ref, dqd_ref, dk_ref, dv_ref,
    dq_out, dk_out, dv_out,
    got, done, ring_send, ring_recv, q_send, q_recv, d_send, g_send, g_recv,
):
    c = lax.axis_index("ctx")
    t = lax.axis_index("tp")
    tokens = dq_out.shape[0]
    width = dq_ref.shape[1]
    thin = dk_ref.shape[1]
    heads = thin // D
    chunk = ctx * tokens
    part = chunk // SUB
    p = ring_place(t, tp)
    after = ring_owner(p + 1, tp)
    before = ring_owner(p - 1, tp)
    origin = meet(c, t, ctx, tp, before, after)
    ways = ((dk_ref, 1, after), (dv_ref, -1, before))

    def own(way, place, sub):
        at = pl.multiple_of(ring_owner(place, tp) * chunk + sub * part, part)
        return ways[way][0].at[pl.ds(at, part), :]

    def hop(way, src, step, sub):
        return remote(
            src, got.at[way, step, sub], ring_send.at[way, step, sub],
            ring_recv.at[way, step, sub], c, ways[way][2],
        )

    for sub in range(SUB):
        for way in range(2):
            hop(way, own(way, p - ways[way][1], sub), 0, sub).start()

    def rows_of(k):
        return dq_ref.at[pl.ds(pl.multiple_of(k * tokens, tokens), tokens), :]

    columns = dq_out.at[:, pl.ds(pl.multiple_of(c * width, width), width)]
    for k in range(1, ctx):
        peer = (c + k) % ctx

        @pl.when(peer * tp + t != 0)
        def send():
            remote(rows_of(peer), columns, q_send.at[k], q_recv, peer, t).start()

    @pl.when(jnp.logical_not(origin))
    def keep_rows():
        pltpu.make_async_copy(rows_of(c), columns, q_recv).start()

    rows = dqd_ref.shape[0]
    first = t * rows
    token = pl.multiple_of(first % T, rows)

    def dense(h):
        column = c * width + h * (GROUP_SIZE * D) + (first // T) * D
        return (
            dqd_ref.at[:, h * D:(h + 1) * D],
            dq_out.at[pl.ds(token, rows), pl.ds(pl.multiple_of(column, D), D)],
        )

    for h in range(heads):
        src, dst = dense(h)

        @pl.when(origin)
        def stay():
            pltpu.make_async_copy(src, dst, q_recv).start()

        @pl.when(jnp.logical_not(origin))
        def leave():
            remote(src, dst, d_send.at[h], q_recv, 0, 0).start()

    def total(way, step, sub):
        hop(way, got.at[way, step, sub], step, sub).wait_recv()
        place = p - ways[way][1] * (step + 2)
        return got[way, step, sub].astype(F32) + own(way, place, sub)[...].astype(F32)

    def advance(step, none):
        for sub in range(SUB):
            for way in range(2):
                got[way, step - 1, sub] = total(way, step - 1, sub).astype(BF16)
                hop(way, got.at[way, step - 1, sub], step, sub).start()
        return none

    lax.fori_loop(1, tp - 1, advance, 0)
    outs = (dk_out, dv_out)

    def give(way, peer, k):
        src = done.at[way, pl.ds(pl.multiple_of(peer * tokens, tokens), tokens), :]
        dst = outs[way].at[:, pl.ds(pl.multiple_of(c * thin, thin), thin)]
        return src, dst

    for sub in range(SUB):
        for way in range(2):
            done[way, sub * part:(sub + 1) * part, :] = total(way, tp - 2, sub).astype(BF16)
    for way in range(2):
        for k in range(1, ctx):
            peer = (c + k) % ctx
            src, dst = give(way, peer, k)
            remote(src, dst, g_send.at[way, k], g_recv.at[way], peer, t).start()
        src, dst = give(way, c, 0)
        pltpu.make_async_copy(src, dst, g_recv.at[way]).start()

    await_bytes(dq_out, q_recv)
    for way in range(2):
        await_bytes(outs[way], g_recv.at[way])
    for way in range(2):
        for k in range(1, ctx):
            peer = (c + k) % ctx
            src, dst = give(way, peer, k)
            remote(src, dst, g_send.at[way, k], g_recv.at[way], peer, t).wait_send()
    for k in range(1, ctx):
        peer = (c + k) % ctx

        @pl.when(peer * tp + t != 0)
        def sent():
            remote(rows_of(peer), columns, q_send.at[k], q_recv, peer, t).wait_send()

    for h in range(heads):
        src, dst = dense(h)

        @pl.when(jnp.logical_not(origin))
        def left():
            remote(src, dst, d_send.at[h], q_recv, 0, 0).wait_send()

    def settle(step, none):
        for sub in range(SUB):
            for way in range(2):
                hop(way, got.at[way, step, sub], step, sub).wait_send()
        return none

    lax.fori_loop(0, tp - 1, settle, 0)


def send_back(dq, dqd, dk, dv, ctx, tp):
    tokens = dq.shape[0] // ctx
    thin = dk.shape[1]
    heads = thin // D
    part = ctx * tokens // SUB
    anywhere = pl.BlockSpec(memory_space=pl.ANY)
    vmem = pl.BlockSpec(memory_space=pltpu.VMEM)
    dma = pltpu.SemaphoreType.DMA
    return pl.pallas_call(
        functools.partial(return_kernel, ctx, tp),
        in_specs=[anywhere, anywhere, vmem, vmem],
        out_specs=[anywhere, anywhere, anywhere],
        out_shape=[
            jax.ShapeDtypeStruct((tokens, ctx * dq.shape[1]), BF16),
            jax.ShapeDtypeStruct((tokens, ctx * thin), BF16),
            jax.ShapeDtypeStruct((tokens, ctx * thin), BF16),
        ],
        scratch_shapes=[
            pltpu.VMEM((2, tp - 1, SUB, part, thin), BF16),
            pltpu.VMEM((2, ctx * tokens, thin), BF16),
            dma((2, tp - 1, SUB)), dma((2, tp - 1, SUB)),
            dma((ctx,)), dma, dma((heads,)), dma((2, ctx)), dma((2,)),
        ],
        compiler_params=pltpu.CompilerParams(
            collective_id=1, has_side_effects=True, vmem_limit_bytes=48 * 1024 * 1024
        ),
    )(dq, dqd, dk, dv)


def exchange_kernel(
    ctx, tp,
    q_ref, o_ref, k_ref, v_ref,
    q_out, o_out, k_out, v_out, qd_out, od_out,
    kv_send, kv_recv, ring_send, ring_recv, qo_send, qo_recv, d_send, d_recv,
):
    c = lax.axis_index("ctx")
    t = lax.axis_index("tp")
    tokens = q_ref.shape[0]
    width = q_out.shape[1]
    thin = k_out.shape[1]
    heads = thin // D
    chunk = ctx * tokens
    part = chunk // SUB
    p = ring_place(t, tp)
    after = ring_owner(p + 1, tp)
    before = ring_owner(p - 1, tp)
    origin = meet(c, t, ctx, tp, before, after)
    thins = ((k_ref, k_out), (v_ref, v_out))
    wides = ((q_ref, q_out), (o_ref, o_out))
    mine = pl.multiple_of(t * chunk + c * tokens, tokens)

    def thin_copy(way, peer):
        src, dst = thins[way]
        return src.at[:, pl.ds(pl.multiple_of(peer * thin, thin), thin)], dst.at[pl.ds(mine, tokens), :]

    for k in range(1, ctx):
        peer = (c + k) % ctx
        for way in range(2):
            src, dst = thin_copy(way, peer)
            remote(src, dst, kv_send.at[way, k], kv_recv.at[way], peer, t).start()
    for way in range(2):
        src, dst = thin_copy(way, c)
        pltpu.make_async_copy(src, dst, kv_recv.at[way]).start()

    def wide_copy(i, peer):
        src, dst = wides[i]
        return (
            src.at[:, pl.ds(pl.multiple_of(peer * width, width), width)],
            dst.at[pl.ds(pl.multiple_of(c * tokens, tokens), tokens), :],
        )

    @pl.when(jnp.logical_not(origin))
    def wide_start():
        for i in range(2):
            for k in range(1, ctx):
                peer = (c + k) % ctx
                src, dst = wide_copy(i, peer)
                remote(src, dst, qo_send.at[i, k], qo_recv.at[i], peer, t).start()
            src, dst = wide_copy(i, c)
            pltpu.make_async_copy(src, dst, qo_recv.at[i]).start()

    rows = qd_out.shape[0]
    dense_outs = (qd_out, od_out)

    def dense(i, h, c_to, t_to):
        first = t_to * rows
        column = c_to * width + h * (GROUP_SIZE * D) + (first // T) * D
        return (
            wides[i][0].at[
                pl.ds(pl.multiple_of(first % T, rows), rows), pl.ds(pl.multiple_of(column, D), D)
            ],
            dense_outs[i].at[:, h * D:(h + 1) * D],
        )

    @pl.when(origin)
    def dense_start():
        def one(n, none):
            for i in range(2):
                for h in range(heads):
                    src, dst = dense(i, h, n // tp, n % tp)
                    remote(src, dst, d_send.at[i], d_recv.at[i], n // tp, n % tp).start()
            return none

        lax.fori_loop(1, ctx * tp, one, 0)
        for i in range(2):
            for h in range(heads):
                src, dst = dense(i, h, 0, 0)
                pltpu.make_async_copy(src, dst, d_recv.at[i]).start()

    def hop(way, step, sub):
        place = p - step if way == 0 else p + step
        at = pl.multiple_of(ring_owner(place, tp) * chunk + sub * part, part)
        ref = thins[way][1].at[pl.ds(at, part), :]
        return remote(
            ref, ref, ring_send.at[way, step, sub], ring_recv.at[way, step, sub],
            c, (after, before)[way],
        )

    for way in range(2):
        at = pl.multiple_of(t * chunk, chunk)
        await_bytes(thins[way][1].at[pl.ds(at, chunk), :], kv_recv.at[way])
        for sub in range(SUB):
            hop(way, 0, sub).start()

    def advance(step, none):
        for sub in range(SUB):
            for way in range(2):
                hop(way, step - 1, sub).wait_recv()
                hop(way, step, sub).start()
        return none

    lax.fori_loop(1, tp - 1, advance, 0)
    for sub in range(SUB):
        for way in range(2):
            hop(way, tp - 2, sub).wait_recv()

    for i in range(2):
        await_bytes(dense_outs[i], d_recv.at[i])

        @pl.when(t == 0)
        def part_rows():
            await_bytes(wides[i][1].at[tokens:, :], qo_recv.at[i])

        @pl.when(t != 0)
        def all_rows():
            await_bytes(wides[i][1], qo_recv.at[i])

    for way in range(2):
        for k in range(1, ctx):
            peer = (c + k) % ctx
            src, dst = thin_copy(way, peer)
            remote(src, dst, kv_send.at[way, k], kv_recv.at[way], peer, t).wait_send()

    @pl.when(jnp.logical_not(origin))
    def wide_sent():
        for i in range(2):
            for k in range(1, ctx):
                peer = (c + k) % ctx
                src, dst = wide_copy(i, peer)
                remote(src, dst, qo_send.at[i, k], qo_recv.at[i], peer, t).wait_send()

    @pl.when(origin)
    def dense_sent():
        def one(n, none):
            for i in range(2):
                await_bytes(dense_outs[i], d_send.at[i])
            return none

        lax.fori_loop(1, ctx * tp, one, 0)

    def settle(step, none):
        for sub in range(SUB):
            for way in range(2):
                hop(way, step, sub).wait_send()
        return none

    lax.fori_loop(0, tp - 1, settle, 0)


def exchange(q, o, k, v, ctx, tp):
    tokens = q.shape[0]
    width = q.shape[1] // ctx
    thin = k.shape[1] // ctx
    rows = GROUP_SIZE * T // tp
    anywhere = pl.BlockSpec(memory_space=pl.ANY)
    dma = pltpu.SemaphoreType.DMA
    shape = lambda *dims: jax.ShapeDtypeStruct(dims, BF16)
    return pl.pallas_call(
        functools.partial(exchange_kernel, ctx, tp),
        in_specs=[anywhere] * 4,
        out_specs=[anywhere] * 6,
        out_shape=[
            shape(ctx * tokens, width), shape(ctx * tokens, width),
            shape(tp * ctx * tokens, thin), shape(tp * ctx * tokens, thin),
            shape(rows, thin), shape(rows, thin),
        ],
        scratch_shapes=[
            dma((2, ctx)), dma((2,)),
            dma((2, tp - 1, SUB)), dma((2, tp - 1, SUB)),
            dma((2, ctx)), dma((2,)), dma((2,)), dma((2,)),
        ],
        compiler_params=pltpu.CompilerParams(
            collective_id=2, has_side_effects=True, vmem_limit_bytes=48 * 1024 * 1024
        ),
    )(q, o, k, v)


def per_device(queries, key_tensor, value_tensor, output_gradient, key_blocks, slot_valid):
    ctx = lax.axis_size("ctx")
    tp = lax.axis_size("tp")
    pieces = queries.shape[0] // T
    table, live, keep = tables(key_blocks, slot_valid, ctx, tp, pieces)
    q, o, k, v, qd, od = exchange(queries, output_gradient, key_tensor, value_tensor, ctx, tp)
    dq, dk, dv, dqd = gradients(table, live, keep, q, o, k, v, qd, od)
    return tuple(send_back(dq, dqd, dk, dv, ctx, tp))


def solution(mesh):
    rows = P(("ctx", "tp"), None)
    return jax.shard_map(
        per_device,
        mesh=mesh,
        in_specs=(rows, rows, rows, rows, P(), P()),
        out_specs=(rows, rows, rows),
        check_vma=False,
    )
```

```python
import functools
import math

import jax
import jax.numpy as jnp
from jax import lax
from jax.experimental import pallas as pl
from jax.experimental.pallas import tpu as pltpu
from jax.sharding import PartitionSpec as P

KEY_HEADS = 8
HEAD_SIZE = 128
BLOCK_TOKENS = 128
NB = 8
GROUP_SIZE = 8
SUB = 2

SCALE = 1.0 / math.sqrt(HEAD_SIZE)
LOG_SCALE = SCALE * math.log2(math.e)
T = BLOCK_TOKENS
D = HEAD_SIZE
F32 = jnp.float32
BF16 = jnp.bfloat16


def dot_nt(a, b):
    return lax.dot_general(a, b, (((1,), (1,)), ((), ())), preferred_element_type=F32)


def dot_nn(a, b):
    return jnp.dot(a, b, preferred_element_type=F32)


def grad_kernel(
    table, live, keep,
    q_ref, o_ref, k_ref, v_ref, qd_ref, od_ref,
    dq_ref, dk_ref, dv_ref, dqd_ref,
    kt, acc_k, acc_v, qs, os_, kg, vg, ktg, s_buf, g_buf, pb, ds,
):
    j = pl.program_id(1)
    length = k_ref.shape[0]
    chunk = math.gcd(length, 512)

    @pl.when(j == 0)
    def dense():
        qd = qd_ref[...]
        od = od_ref[...]
        rows = qd.shape[0]

        def stats(i, carry):
            m, l, dl = carry
            at = pl.multiple_of(i * chunk, chunk)
            k = k_ref[pl.ds(at, chunk), :]
            s = dot_nt(k, qd) * LOG_SCALE
            g = dot_nt(v_ref[pl.ds(at, chunk), :], od)
            kt[:, pl.ds(at, chunk)] = k.T
            m_new = jnp.maximum(m, jnp.max(s, axis=0, keepdims=True))
            f = jnp.exp2(m - m_new)
            p = jnp.exp2(s - m_new)
            l = l * f + jnp.sum(p, axis=0, keepdims=True)
            dl = dl * f + jnp.sum(p * g, axis=0, keepdims=True)
            return m_new, l, dl

        m, l, dl = lax.fori_loop(
            0, length // chunk, stats,
            (jnp.full((1, rows), -1e30, F32), jnp.zeros((1, rows), F32), jnp.zeros((1, rows), F32)),
        )
        rl = 1.0 / l
        delta = dl * rl

        def grads(i, dqt):
            at = pl.multiple_of(i * chunk, chunk)
            s = dot_nt(k_ref[pl.ds(at, chunk), :], qd) * LOG_SCALE
            g = dot_nt(v_ref[pl.ds(at, chunk), :], od)
            p = jnp.exp2(s - m) * rl
            d = (p * (g - delta)).astype(BF16)
            acc_v[pl.ds(at, chunk), :] = dot_nn(p.astype(BF16), od)
            acc_k[pl.ds(at, chunk), :] = dot_nn(d, qd)
            return dqt + dot_nn(kt[:, pl.ds(at, chunk)], d)

        dqt = lax.fori_loop(0, length // chunk, grads, jnp.zeros((D, rows), F32))
        dqd_ref[...] = (dqt * SCALE).T.astype(BF16)

    @pl.when(keep[j] == 0)
    def blank():
        dq_ref[...] = jnp.zeros_like(dq_ref)

    @pl.when(keep[j] != 0)
    def sparse():
        for g in range(GROUP_SIZE):
            qs[g * T:(g + 1) * T, :] = q_ref[:, g * D:(g + 1) * D]
            os_[g * T:(g + 1) * T, :] = o_ref[:, g * D:(g + 1) * D]
        bias = []
        for s in range(NB):
            at = pl.multiple_of(table[j * NB + s] * T, T)
            kg[s * T:(s + 1) * T, :] = k_ref[pl.ds(at, T), :]
            vg[s * T:(s + 1) * T, :] = v_ref[pl.ds(at, T), :]
            ktg[:, s * T:(s + 1) * T] = kt[:, pl.ds(at, T)]
            bias.append(jnp.where(live[j * NB + s] > 0, 0.0, -1e30).astype(F32))
        R = 2 * T
        for pair in range(GROUP_SIZE // 2):
            q2 = qs[pair * R:(pair + 1) * R, :]
            o2 = os_[pair * R:(pair + 1) * R, :]
            m = None
            for s in range(NB):
                sc = dot_nt(kg[s * T:(s + 1) * T, :], q2)
                s_buf[s * T:(s + 1) * T, :] = sc
                top = jnp.max(sc, axis=0, keepdims=True) * LOG_SCALE + bias[s]
                m = top if m is None else jnp.maximum(m, top)
            l = jnp.zeros((1, R), F32)
            dl = jnp.zeros((1, R), F32)
            for s in range(NB):
                rows = slice(s * T, (s + 1) * T)
                p = jnp.exp2(s_buf[rows, :] * LOG_SCALE - (m - bias[s]))
                g = dot_nt(vg[rows, :], o2)
                l = l + jnp.sum(p, axis=0, keepdims=True)
                dl = dl + jnp.sum(p * g, axis=0, keepdims=True)
                s_buf[rows, :] = p
                g_buf[rows, :] = g
            rl = 1.0 / l
            delta = dl * rl
            cols = slice(pair * R, (pair + 1) * R)
            for s in range(NB):
                rows = slice(s * T, (s + 1) * T)
                p = s_buf[rows, :] * rl
                pb[rows, cols] = p.astype(BF16)
                ds[rows, cols] = (p * (g_buf[rows, :] - delta)).astype(BF16)
            dqt = dot_nn(ktg[...], ds[:, cols]) * SCALE
            dq_ref[:, 2 * pair * D:(2 * pair + 1) * D] = dqt[:, :T].T.astype(BF16)
            dq_ref[:, (2 * pair + 1) * D:(2 * pair + 2) * D] = dqt[:, T:].T.astype(BF16)
        for s in range(NB):
            rows = slice(s * T, (s + 1) * T)
            at = pl.multiple_of(table[j * NB + s] * T, T)
            acc_v[pl.ds(at, T), :] += dot_nn(pb[rows, :], os_[...])
            acc_k[pl.ds(at, T), :] += dot_nn(ds[rows, :], qs[...])

    @pl.when(j == pl.num_programs(1) - 1)
    def finish():
        dk_ref[...] = (acc_k[...] * SCALE).astype(BF16)
        dv_ref[...] = acc_v[...].astype(BF16)


def gradients(table, live, keep, q, o, k, v, qd, od):
    blocks = table.shape[0]
    length = k.shape[0]
    heads = k.shape[1] // D
    rows = qd.shape[0]
    wide = GROUP_SIZE * D
    spec = lambda shape, index: pl.BlockSpec(shape, index)
    row_block = spec((T, wide), lambda h, j, *_: (j, h))
    once = pl.Buffered(1) if heads == 1 else None
    fixed = lambda index: pl.BlockSpec((length, D), index, pipeline_mode=once)
    dense = spec((rows, D), lambda h, j, *_: (0, h))
    return pl.pallas_call(
        grad_kernel,
        grid_spec=pltpu.PrefetchScalarGridSpec(
            num_scalar_prefetch=3,
            grid=(heads, blocks),
            in_specs=[
                row_block, row_block,
                fixed(lambda h, j, *_: (0, h)),
                fixed(lambda h, j, *_: (0, h)),
                dense, dense,
            ],
            out_specs=[
                row_block,
                spec((length, D), lambda h, j, *_: (0, h)),
                spec((length, D), lambda h, j, *_: (0, h)),
                dense,
            ],
            scratch_shapes=[
                pltpu.VMEM((D, length), BF16),
                pltpu.VMEM((length, D), F32),
                pltpu.VMEM((length, D), F32),
                pltpu.VMEM((wide, D), BF16),
                pltpu.VMEM((wide, D), BF16),
                pltpu.VMEM((NB * T, D), BF16),
                pltpu.VMEM((NB * T, D), BF16),
                pltpu.VMEM((D, NB * T), BF16),
                pltpu.VMEM((NB * T, 2 * T), F32),
                pltpu.VMEM((NB * T, 2 * T), F32),
                pltpu.VMEM((NB * T, wide), BF16),
                pltpu.VMEM((NB * T, wide), BF16),
            ],
        ),
        out_shape=[
            jax.ShapeDtypeStruct(q.shape, BF16),
            jax.ShapeDtypeStruct((length, heads * D), BF16),
            jax.ShapeDtypeStruct((length, heads * D), BF16),
            jax.ShapeDtypeStruct(qd.shape, BF16),
        ],
        compiler_params=pltpu.CompilerParams(
            dimension_semantics=("arbitrary", "arbitrary"),
            vmem_limit_bytes=60 * 1024 * 1024,
        ),
        cost_estimate=pl.CostEstimate(
            flops=10 * heads * (blocks + 1) * (wide * NB * T * D),
            bytes_accessed=6 * q.size + 8 * k.size,
            transcendentals=heads * (blocks + 1) * wide * NB * T,
        ),
    )(table.reshape(-1), live.reshape(-1), keep, q, o, k, v, qd, od)


def tables(key_blocks, slot_valid, ctx, tp, pieces):
    t = lax.axis_index("tp")
    pick = lambda a: lax.dynamic_slice_in_dim(
        a.reshape(ctx, tp * pieces, NB), t * pieces, pieces, 1
    ).reshape(ctx * pieces, NB)
    blocks = pick(key_blocks)
    owner = blocks // pieces
    place = ((owner % tp) * ctx + owner // tp) * pieces + blocks % pieces
    number = jnp.arange(ctx * pieces)
    own = ((number // pieces) * tp + t) * pieces + number % pieces
    return place.astype(jnp.int32), pick(slot_valid), (own != 0).astype(jnp.int32)


def ring_place(t, n):
    odd = t % 2
    return (1 - odd) * (t // 2) + odd * (n - 1 - t // 2)


def ring_owner(p, n):
    p = (p + 2 * n) % n
    far = p // (n // 2)
    return (1 - far) * 2 * p + far * (2 * (n - 1 - p) + 1)


def signal(sem, c, t):
    pl.semaphore_signal(sem, inc=1, device_id=(c, t), device_id_type=pl.DeviceIdType.MESH)


def meet(c, t, ctx, tp, before, after, spread):
    barrier = pltpu.get_barrier_semaphore()
    for k in range(1, ctx):
        signal(barrier, (c + k) % ctx, t)
    signal(barrier, c, before)
    signal(barrier, c, after)
    hub_c = 0 if spread else c
    hub = (c * tp + t == 0) if spread else (t == 0)
    count = ctx * tp if spread else tp

    @pl.when(hub)
    def greet():
        def one(i, none):
            signal(barrier, i // tp if spread else c, i % tp)
            return none

        lax.fori_loop(1, count, one, 0)
        pl.semaphore_wait(barrier, ctx + 1 + count - 1)

    @pl.when(jnp.logical_not(hub))
    def answer():
        signal(barrier, hub_c, 0)
        pl.semaphore_wait(barrier, ctx + 2)

    return hub


def remote(src, dst, send, recv, c, t):
    return pltpu.make_async_remote_copy(
        src_ref=src, dst_ref=dst, send_sem=send, recv_sem=recv,
        device_id=(c, t), device_id_type=pl.DeviceIdType.MESH,
    )


def await_bytes(ref, sem):
    pltpu.make_async_copy(ref, ref, sem).wait()


def return_kernel(
    ctx, tp,
    dq_ref, dqd_ref, dk_ref, dv_ref,
    dq_out, dk_out, dv_out,
    got, done, ring_send, ring_recv, q_send, q_recv, d_send, g_send, g_recv,
):
    c = lax.axis_index("ctx")
    t = lax.axis_index("tp")
    tokens = dq_out.shape[0]
    width = dq_ref.shape[1]
    thin = dk_ref.shape[1]
    heads = thin // D
    chunk = ctx * tokens
    part = chunk // SUB
    p = ring_place(t, tp)
    after = ring_owner(p + 1, tp)
    before = ring_owner(p - 1, tp)
    origin = meet(c, t, ctx, tp, before, after, True)
    ways = ((dk_ref, 1, after), (dv_ref, -1, before))

    def own(way, place, sub):
        at = pl.multiple_of(ring_owner(place, tp) * chunk + sub * part, part)
        return ways[way][0].at[pl.ds(at, part), :]

    def hop(way, src, step, sub):
        return remote(
            src, got.at[way, step, sub], ring_send.at[way, step, sub],
            ring_recv.at[way, step, sub], c, ways[way][2],
        )

    for sub in range(SUB):
        for way in range(2):
            hop(way, own(way, p - ways[way][1], sub), 0, sub).start()

    def rows_of(k):
        return dq_ref.at[pl.ds(pl.multiple_of(k * tokens, tokens), tokens), :]

    columns = dq_out.at[:, pl.ds(pl.multiple_of(c * width, width), width)]
    for k in range(1, ctx):
        peer = (c + k) % ctx

        @pl.when(peer * tp + t != 0)
        def send():
            remote(rows_of(peer), columns, q_send.at[k], q_recv, peer, t).start()

    @pl.when(jnp.logical_not(origin))
    def keep_rows():
        pltpu.make_async_copy(rows_of(c), columns, q_recv).start()

    rows = dqd_ref.shape[0]
    first = t * rows
    token = pl.multiple_of(first % T, rows)

    def dense(h):
        column = c * width + h * (GROUP_SIZE * D) + (first // T) * D
        return (
            dqd_ref.at[:, h * D:(h + 1) * D],
            dq_out.at[pl.ds(token, rows), pl.ds(pl.multiple_of(column, D), D)],
        )

    for h in range(heads):
        src, dst = dense(h)

        @pl.when(origin)
        def stay():
            pltpu.make_async_copy(src, dst, q_recv).start()

        @pl.when(jnp.logical_not(origin))
        def leave():
            remote(src, dst, d_send.at[h], q_recv, 0, 0).start()

    def total(way, step, sub):
        hop(way, got.at[way, step, sub], step, sub).wait_recv()
        place = p - ways[way][1] * (step + 2)
        return got[way, step, sub].astype(F32) + own(way, place, sub)[...].astype(F32)

    def advance(step, none):
        for sub in range(SUB):
            for way in range(2):
                got[way, step - 1, sub] = total(way, step - 1, sub).astype(BF16)
                hop(way, got.at[way, step - 1, sub], step, sub).start()
        return none

    lax.fori_loop(1, tp - 1, advance, 0)
    outs = (dk_out, dv_out)

    def give(way, peer, k):
        src = done.at[way, pl.ds(pl.multiple_of(peer * tokens, tokens), tokens), :]
        dst = outs[way].at[:, pl.ds(pl.multiple_of(c * thin, thin), thin)]
        return src, dst

    for sub in range(SUB):
        for way in range(2):
            done[way, sub * part:(sub + 1) * part, :] = total(way, tp - 2, sub).astype(BF16)
    for way in range(2):
        for k in range(1, ctx):
            peer = (c + k) % ctx
            src, dst = give(way, peer, k)
            remote(src, dst, g_send.at[way, k], g_recv.at[way], peer, t).start()
        src, dst = give(way, c, 0)
        pltpu.make_async_copy(src, dst, g_recv.at[way]).start()

    await_bytes(dq_out, q_recv)
    for way in range(2):
        await_bytes(outs[way], g_recv.at[way])
    for way in range(2):
        for k in range(1, ctx):
            peer = (c + k) % ctx
            src, dst = give(way, peer, k)
            remote(src, dst, g_send.at[way, k], g_recv.at[way], peer, t).wait_send()
    for k in range(1, ctx):
        peer = (c + k) % ctx

        @pl.when(peer * tp + t != 0)
        def sent():
            remote(rows_of(peer), columns, q_send.at[k], q_recv, peer, t).wait_send()

    for h in range(heads):
        src, dst = dense(h)

        @pl.when(jnp.logical_not(origin))
        def left():
            remote(src, dst, d_send.at[h], q_recv, 0, 0).wait_send()

    def settle(step, none):
        for sub in range(SUB):
            for way in range(2):
                hop(way, got.at[way, step, sub], step, sub).wait_send()
        return none

    lax.fori_loop(0, tp - 1, settle, 0)


def send_back(dq, dqd, dk, dv, ctx, tp):
    tokens = dq.shape[0] // ctx
    thin = dk.shape[1]
    heads = thin // D
    part = ctx * tokens // SUB
    anywhere = pl.BlockSpec(memory_space=pl.ANY)
    vmem = pl.BlockSpec(memory_space=pltpu.VMEM)
    dma = pltpu.SemaphoreType.DMA
    return pl.pallas_call(
        functools.partial(return_kernel, ctx, tp),
        in_specs=[anywhere, anywhere, vmem, vmem],
        out_specs=[anywhere, anywhere, anywhere],
        out_shape=[
            jax.ShapeDtypeStruct((tokens, ctx * dq.shape[1]), BF16),
            jax.ShapeDtypeStruct((tokens, ctx * thin), BF16),
            jax.ShapeDtypeStruct((tokens, ctx * thin), BF16),
        ],
        scratch_shapes=[
            pltpu.VMEM((2, tp - 1, SUB, part, thin), BF16),
            pltpu.VMEM((2, ctx * tokens, thin), BF16),
            dma((2, tp - 1, SUB)), dma((2, tp - 1, SUB)),
            dma((ctx,)), dma, dma((heads,)), dma((2, ctx)), dma((2,)),
        ],
        compiler_params=pltpu.CompilerParams(
            collective_id=1, has_side_effects=True, vmem_limit_bytes=48 * 1024 * 1024
        ),
    )(dq, dqd, dk, dv)


def exchange_kernel(
    ctx, tp,
    q_ref, o_ref, k_ref, v_ref,
    q_out, o_out, k_out, v_out, qd_out, od_out,
    kv_send, kv_recv, ring_send, ring_recv, qo_send, qo_recv, d_send, d_recv,
):
    c = lax.axis_index("ctx")
    t = lax.axis_index("tp")
    tokens = q_ref.shape[0]
    width = q_out.shape[1]
    thin = k_out.shape[1]
    heads = thin // D
    chunk = ctx * tokens
    part = chunk // SUB
    p = ring_place(t, tp)
    after = ring_owner(p + 1, tp)
    before = ring_owner(p - 1, tp)
    hub = meet(c, t, ctx, tp, before, after, False)
    thins = ((k_ref, k_out), (v_ref, v_out))
    wides = ((q_ref, q_out), (o_ref, o_out))
    mine = pl.multiple_of(t * chunk + c * tokens, tokens)

    def thin_copy(way, peer):
        src, dst = thins[way]
        return src.at[:, pl.ds(pl.multiple_of(peer * thin, thin), thin)], dst.at[pl.ds(mine, tokens), :]

    for k in range(1, ctx):
        peer = (c + k) % ctx
        for way in range(2):
            src, dst = thin_copy(way, peer)
            remote(src, dst, kv_send.at[way, k], kv_recv.at[way], peer, t).start()
    for way in range(2):
        src, dst = thin_copy(way, c)
        pltpu.make_async_copy(src, dst, kv_recv.at[way]).start()

    def wide_copy(i, peer):
        src, dst = wides[i]
        return (
            src.at[:, pl.ds(pl.multiple_of(peer * width, width), width)],
            dst.at[pl.ds(pl.multiple_of(c * tokens, tokens), tokens), :],
        )

    for i in range(2):
        for k in range(1, ctx):
            peer = (c + k) % ctx
            src, dst = wide_copy(i, peer)
            remote(src, dst, qo_send.at[i, k], qo_recv.at[i, c], peer, t).start()
        src, dst = wide_copy(i, c)
        pltpu.make_async_copy(src, dst, qo_recv.at[i, c]).start()

    rows = qd_out.shape[0]
    dense_outs = (qd_out, od_out)

    def dense(i, h, t_to):
        first = t_to * rows
        column = h * (GROUP_SIZE * D) + (first // T) * D
        return (
            wides[i][1].at[
                pl.ds(pl.multiple_of(first % T, rows), rows), pl.ds(pl.multiple_of(column, D), D)
            ],
            dense_outs[i].at[:, h * D:(h + 1) * D],
        )

    def hop(way, step, sub):
        place = p - step if way == 0 else p + step
        at = pl.multiple_of(ring_owner(place, tp) * chunk + sub * part, part)
        ref = thins[way][1].at[pl.ds(at, part), :]
        return remote(
            ref, ref, ring_send.at[way, step, sub], ring_recv.at[way, step, sub],
            c, (after, before)[way],
        )

    for way in range(2):
        at = pl.multiple_of(t * chunk, chunk)
        await_bytes(thins[way][1].at[pl.ds(at, chunk), :], kv_recv.at[way])
        for sub in range(SUB):
            hop(way, 0, sub).start()

    def advance(step, none):
        for sub in range(SUB):
            for way in range(2):
                hop(way, step - 1, sub).wait_recv()
                hop(way, step, sub).start()
        return none

    lax.fori_loop(1, tp - 1, advance, 0)
    for sub in range(SUB):
        for way in range(2):
            hop(way, tp - 2, sub).wait_recv()

    for i in range(2):
        await_bytes(wides[i][1].at[:tokens, :], qo_recv.at[i, 0])

    @pl.when(hub)
    def dense_start():
        def one(n, none):
            for i in range(2):
                for h in range(heads):
                    src, dst = dense(i, h, n)
                    remote(src, dst, d_send.at[i], d_recv.at[i], c, n).start()
            return none

        lax.fori_loop(1, tp, one, 0)
        for i in range(2):
            for h in range(heads):
                src, dst = dense(i, h, 0)
                pltpu.make_async_copy(src, dst, d_recv.at[i]).start()

    for i in range(2):
        for k in range(1, ctx):
            await_bytes(wides[i][1].at[k * tokens:(k + 1) * tokens, :], qo_recv.at[i, k])
    for i in range(2):
        await_bytes(dense_outs[i], d_recv.at[i])

    for way in range(2):
        for k in range(1, ctx):
            peer = (c + k) % ctx
            src, dst = thin_copy(way, peer)
            remote(src, dst, kv_send.at[way, k], kv_recv.at[way], peer, t).wait_send()

    for i in range(2):
        for k in range(1, ctx):
            peer = (c + k) % ctx
            src, dst = wide_copy(i, peer)
            remote(src, dst, qo_send.at[i, k], qo_recv.at[i, c], peer, t).wait_send()

    @pl.when(hub)
    def dense_sent():
        def one(n, none):
            for i in range(2):
                await_bytes(dense_outs[i], d_send.at[i])
            return none

        lax.fori_loop(1, tp, one, 0)

    def settle(step, none):
        for sub in range(SUB):
            for way in range(2):
                hop(way, step, sub).wait_send()
        return none

    lax.fori_loop(0, tp - 1, settle, 0)


def exchange(q, o, k, v, ctx, tp):
    tokens = q.shape[0]
    width = q.shape[1] // ctx
    thin = k.shape[1] // ctx
    rows = GROUP_SIZE * T // tp
    anywhere = pl.BlockSpec(memory_space=pl.ANY)
    dma = pltpu.SemaphoreType.DMA
    shape = lambda *dims: jax.ShapeDtypeStruct(dims, BF16)
    return pl.pallas_call(
        functools.partial(exchange_kernel, ctx, tp),
        in_specs=[anywhere] * 4,
        out_specs=[anywhere] * 6,
        out_shape=[
            shape(ctx * tokens, width), shape(ctx * tokens, width),
            shape(tp * ctx * tokens, thin), shape(tp * ctx * tokens, thin),
            shape(rows, thin), shape(rows, thin),
        ],
        scratch_shapes=[
            dma((2, ctx)), dma((2,)),
            dma((2, tp - 1, SUB)), dma((2, tp - 1, SUB)),
            dma((2, ctx)), dma((2, ctx)), dma((2,)), dma((2,)),
        ],
        compiler_params=pltpu.CompilerParams(
            collective_id=2, has_side_effects=True, vmem_limit_bytes=48 * 1024 * 1024
        ),
    )(q, o, k, v)


def per_device(queries, key_tensor, value_tensor, output_gradient, key_blocks, slot_valid):
    ctx = lax.axis_size("ctx")
    tp = lax.axis_size("tp")
    pieces = queries.shape[0] // T
    table, live, keep = tables(key_blocks, slot_valid, ctx, tp, pieces)
    q, o, k, v, qd, od = exchange(queries, output_gradient, key_tensor, value_tensor, ctx, tp)
    dq, dk, dv, dqd = gradients(table, live, keep, q, o, k, v, qd, od)
    return tuple(send_back(dq, dqd, dk, dv, ctx, tp))


def solution(mesh):
    rows = P(("ctx", "tp"), None)
    return jax.shard_map(
        per_device,
        mesh=mesh,
        in_specs=(rows, rows, rows, rows, P(), P()),
        out_specs=(rows, rows, rows),
        check_vma=False,
    )
```
